32 devices in a mesh: dp: 4 (over x, core), tx: 4 (over z), ty: 2 (over y).
Axes of the slice: x: 2, y: 2, z: 4, core: 2. Of those that a mesh axis runs over, the one named last changes fastest.
Arguments:
- frames: bfloat16 [4, 3072, 1024], P('dp', ('tx', 'ty')), may hold values from -6 to 6
- first_conv_weight: bfloat16 [1024, 4096], replicated, may hold values from -0.125 to 0.125
- first_residual_projection: bfloat16 [1024, 1024], replicated, may hold values from -0.1875 to 0.1875
- second_conv_weight: bfloat16 [1024, 4096], replicated, may hold values from -0.125 to 0.125
- second_residual_projection: bfloat16 [1024, 1024], replicated, may hold values from -0.1875 to 0.1875
- out_grad: bfloat16 [4, 3072, 1024], P('dp', ('tx', 'ty')), may hold values from -6 to 6
Outputs:
- output_frames: bfloat16 [4, 3072, 1024], P('dp', ('tx', 'ty'))
- frame_grad: bfloat16 [4, 3072, 1024], P('dp', ('tx', 'ty'))
- conv_first_grad: float32 [1024, 4096], P('ty')
- proj_first_grad: float32 [1024, 1024], P('ty')
- conv_second_grad: float32 [1024, 4096], P('ty')
- proj_second_grad: float32 [1024, 1024], P('ty')
The draws below stay inside these ranges and needn't reach their ends.
All inputs are finite; a program needn't handle non-finite values.
Results may differ from the reference program's by a relative error of at most 0.023.
Values may be sent and summed in bfloat16 or wider, within the bound.
No kernel may reach another device: no remote copies, remote signals or barrier semaphores. Data moves between devices by JAX's collectives and lax.ppermute only.
A program may use at most 128 MiB of HBM per device.

```python
import jax
import jax.numpy as jnp
from jax import lax

CHANNELS = 1024
FRAMES_DEV = 384
NEAR_DILATION = 64
FAR_DILATION = 768
STREAM_LEN = 3072
STREAMS = 4


def raised(values, stream_key, source, target, shards_of, factor):
    def block_of(dim):
        return (jnp.arange(values.shape[dim]) // (values.shape[dim] // shards_of)).reshape((-1,) + (1,) * (values.ndim - 1 - dim))

    one_side = jax.random.permutation(stream_key, shards_of)[block_of(target)]
    far = (block_of(target) + shards_of // 2) % shards_of
    return jnp.where((block_of(source) == one_side) | (block_of(source) == far), factor * values, values)


def steps_of(key, dims, cuts, low, largest):
    gain = 1.0
    for dim, shards_of in cuts:
        heights = jax.random.uniform(jax.random.fold_in(jax.random.fold_in(key, 6), dim), (shards_of,), jnp.float32, low / len(cuts), largest / len(cuts))
        gain = gain * jnp.repeat(jnp.exp(heights), dims[dim] // shards_of).reshape((-1,) + (1,) * (len(dims) - 1 - dim))
    return gain


def bell_draw(rng, shape, width, reach, cuts=(), kind=jnp.bfloat16):
    level = steps_of(rng, shape, cuts, -0.22, 0.18) if cuts else 1.0
    array = jax.random.normal(rng, shape, jnp.float32) * width * level
    return jnp.minimum(jnp.maximum(array, -reach), reach).astype(kind)


def bell_draw_with(rng, extent, spread, bound, shards, heavy, held_as=jnp.bfloat16):
    array = spread * jax.random.normal(rng, extent, jnp.float32)
    if shards:
        array = array * steps_of(rng, extent, shards, -0.22, 0.18)
    return jnp.clip(raised(array, jax.random.fold_in(rng, 3), *heavy), -bound, bound).astype(held_as)


def setup_inputs(seed: int = 0) -> dict:
    seeds = jax.random.split(jax.random.key(seed), 7)
    return {
        "frames": bell_draw_with(seeds[0], (STREAMS, STREAM_LEN, CHANNELS), 1.0, 6.0, ((0, 4), (1, 8)), (1, 2, 8, 2.0)),
        "first_conv_weight": bell_draw(seeds[1], (CHANNELS, 4 * CHANNELS), (2 * CHANNELS) ** -0.5, 0.125),
        "first_residual_projection": bell_draw(seeds[2], (CHANNELS, CHANNELS), CHANNELS ** -0.5, 0.1875),
        "second_conv_weight": bell_draw(seeds[3], (CHANNELS, 4 * CHANNELS), (2 * CHANNELS) ** -0.5, 0.125),
        "second_residual_projection": bell_draw(seeds[4], (CHANNELS, CHANNELS), CHANNELS ** -0.5, 0.1875),
        "out_grad": bell_draw(seeds[5], (STREAMS, STREAM_LEN, CHANNELS), 1.0, 6.0, ((0, 4), (1, 8))),
    }


def delay_rows(value_rows, dilation):
    return jnp.concatenate([jnp.zeros((dilation, value_rows.shape[1]), value_rows.dtype), value_rows[:-dilation]], 0)


def advance_rows(value_rows, dilation):
    return jnp.concatenate([value_rows[dilation:], jnp.zeros((dilation, value_rows.shape[1]), value_rows.dtype)], 0)


def forward_layer_pass(input_frames, conv_weight, proj_weight, dilation):
    shifted = delay_rows(input_frames, dilation)
    pre = jnp.dot(shifted, conv_weight[:, :2 * CHANNELS], preferred_element_type=jnp.float32)
    pre = pre + jnp.dot(input_frames, conv_weight[:, 2 * CHANNELS:], preferred_element_type=jnp.float32)
    tanh_part = jnp.tanh(pre[:, :CHANNELS])
    gate_part = jax.nn.sigmoid(pre[:, CHANNELS:])
    gated = (tanh_part * gate_part).astype(jnp.bfloat16)
    output = (input_frames.astype(jnp.float32) + jnp.dot(gated, proj_weight, preferred_element_type=jnp.float32)).astype(jnp.bfloat16)
    return output, shifted, tanh_part, gate_part, gated


def backward_layer_pass(tanh_part, gate_part, grad_out, conv_weight, proj_weight, dilation):
    grad_gated = jnp.dot(grad_out, proj_weight.T, preferred_element_type=jnp.float32)
    grad_pre = jnp.concatenate([grad_gated * gate_part * (1.0 - tanh_part * tanh_part),
                                grad_gated * tanh_part * gate_part * (1.0 - gate_part)], 1).astype(jnp.bfloat16)
    tap_part = jnp.dot(grad_pre, conv_weight[:, :2 * CHANNELS].T, preferred_element_type=jnp.float32).astype(jnp.bfloat16)
    grad_in = grad_out.astype(jnp.float32) + jnp.dot(grad_pre, conv_weight[:, 2 * CHANNELS:].T, preferred_element_type=jnp.float32)
    grad_in = (grad_in + advance_rows(tap_part, dilation).astype(jnp.float32)).astype(jnp.bfloat16)
    return grad_in, grad_pre


def block_partials(shifted, input_frames, grad_pre, gated, grad_out):
    blocks = STREAM_LEN // FRAMES_DEV

    def split(value_rows):
        return value_rows.reshape(blocks, FRAMES_DEV, value_rows.shape[1])

    def advance(running, pieces):
        piece_shift, piece_in, piece_pre, piece_gated, piece_out = pieces
        term = jnp.concatenate([jnp.dot(piece_shift.T, piece_pre, preferred_element_type=jnp.float32),
                                jnp.dot(piece_in.T, piece_pre, preferred_element_type=jnp.float32),
                                jnp.dot(piece_gated.T, piece_out, preferred_element_type=jnp.float32)], 1)
        rounded = lax.optimization_barrier(term.astype(jnp.bfloat16))
        return running + rounded.astype(jnp.float32), None

    block_input = jnp.zeros((CHANNELS, 5 * CHANNELS), jnp.float32)
    running, unused = lax.scan(advance, block_input, (split(shifted), split(input_frames), split(grad_pre), split(gated), split(grad_out)))
    return running


def reference(frames, first_conv_weight, first_residual_projection, second_conv_weight, second_residual_projection, out_grad):
    def one_stream(stream_pair):
        block_input, output_gradient = stream_pair
        middle_activation, first_shifted_input, first_tanh_filter, first_gate, first_gated_value = forward_layer_pass(block_input, first_conv_weight, first_residual_projection, NEAR_DILATION)
        block_output, second_shifted_input, second_tanh_filter, second_gate, second_gated_value = forward_layer_pass(middle_activation, second_conv_weight, second_residual_projection, FAR_DILATION)
        middle_gradient, second_preactivation = backward_layer_pass(second_tanh_filter, second_gate, output_gradient, second_conv_weight, second_residual_projection, FAR_DILATION)
        input_gradient, first_preactivation = backward_layer_pass(first_tanh_filter, first_gate, middle_gradient, first_conv_weight, first_residual_projection, NEAR_DILATION)
        total_two = block_partials(second_shifted_input, middle_activation, second_preactivation, second_gated_value, output_gradient)
        total_one = block_partials(first_shifted_input, block_input, first_preactivation, first_gated_value, middle_gradient)
        return block_output, input_gradient, total_one, total_two

    finals, grads, totals_one, totals_two = lax.map(one_stream, (frames, out_grad))
    scale = float(STREAMS * STREAM_LEN) ** -0.5
    total_one = jnp.sum(totals_one, 0) * scale
    total_two = jnp.sum(totals_two, 0) * scale
    return (finals, grads, total_one[:, :4 * CHANNELS], total_one[:, 4 * CHANNELS:],
            total_two[:, :4 * CHANNELS], total_two[:, 4 * CHANNELS:])
```

```python
import jax
import jax.numpy as jnp
from jax import lax
from jax.sharding import Mesh
from jax.sharding import PartitionSpec as P

NEAR_DILATION = 64
BF16 = jnp.bfloat16
F32 = jnp.float32


def shifted_by(value, axis, steps):
    count = lax.axis_size(axis)
    leading, last = (max(0, -steps), min(count, count - steps))
    return lax.ppermute(value, axis, [(source, source + steps) for source in range(leading, last)])


def from_pair(value):
    return lax.ppermute(value, "dc", [(0, 1), (1, 0)])


def mult_trans(left, right):
    return lax.dot_general(left, right, (((1,), (1,)), ((), ())), preferred_element_type=F32)


def contract_rows(left, right):
    return lax.dot_general(left, right, (((0,), (0,)), ((), ())), preferred_element_type=F32)


def causal_parts(input_frames, shifted, conv_weight, proj_weight):
    width = input_frames.shape[1]
    pre = jnp.dot(shifted, conv_weight[:, : 2 * width], preferred_element_type=F32)
    pre = pre + jnp.dot(input_frames, conv_weight[:, 2 * width :], preferred_element_type=F32)
    tanh_part = jnp.tanh(pre[:, :width])
    gate_part = jax.nn.sigmoid(pre[:, width:])
    gated = (tanh_part * gate_part).astype(BF16)
    output = (
        input_frames.astype(F32) + jnp.dot(gated, proj_weight, preferred_element_type=F32)
    ).astype(BF16)
    return (output, tanh_part, gate_part, gated)


def grad_halves(tanh_part, gate_part, grad_out, proj_weight):
    grad_gated = mult_trans(grad_out, proj_weight)
    tanh_half = (grad_gated * gate_part * (1.0 - tanh_part * tanh_part)).astype(BF16)
    gate_half = (grad_gated * tanh_part * gate_part * (1.0 - gate_part)).astype(BF16)
    return tanh_half, gate_half


def halves_of(core, first, second):
    return jnp.where(core == 0, first, second), jnp.where(core == 0, second, first)


def row_share(pieces, axis):
    if lax.axis_size(axis) != 2:
        return lax.psum_scatter(pieces, axis, scatter_dimension=0, tiled=False)
    place = lax.axis_index(axis)
    sent = lax.dynamic_index_in_dim(pieces, 1 - place, 0, keepdims=False)
    kept = lax.dynamic_index_in_dim(pieces, place, 0, keepdims=False)
    came = lax.ppermute(sent, axis, [(0, 1), (1, 0)])
    return (kept.astype(F32) + came.astype(F32)).astype(BF16)


def sum_early(term):
    shares = lax.axis_size("ty")
    parts = lax.axis_size(("dx", "tx"))
    rows = term.shape[0] // shares
    share = row_share(term.reshape(shares, rows, term.shape[1]), "ty")
    share = share.reshape(parts, rows // parts, term.shape[1])
    return lax.psum_scatter(share, ("dx", "tx"), scatter_dimension=0, tiled=False)


def sum_late(term):
    shares = lax.axis_size("ty")
    parts = lax.axis_size(("dx", "tx"))
    rows = term.shape[0] // (shares * parts)
    cut = term.reshape(shares, parts, rows, term.shape[1]).transpose(1, 0, 2, 3)
    piece = lax.psum_scatter(cut, ("dx", "tx"), scatter_dimension=0, tiled=False)
    return row_share(piece, "ty")


def gather_rows(tap, rest):
    whole = lax.all_gather(jnp.concatenate([tap, rest], 1), ("dx", "tx"), axis=0, tiled=True)
    return whole


def finish(core, scale, mine, width):
    other = from_pair(mine)
    first, second = halves_of(core, mine, other)
    conv = jnp.concatenate(
        [first[:, :width], second[:, :width], first[:, width : 2 * width], second[:, width : 2 * width]], 1
    )
    proj = jnp.concatenate([first[:, 2 * width :], second[:, 2 * width :]], 1)
    return conv.astype(F32) * scale, proj.astype(F32) * scale


def shards(
    frames,
    first_conv_weight,
    first_residual_projection,
    second_conv_weight,
    second_residual_projection,
    out_grad,
):
    near = NEAR_DILATION
    block_input = frames[0]
    output_gradient = out_grad[0]
    rows, width = block_input.shape
    half = width // 2
    core = lax.axis_index("dc")
    far_steps = lax.axis_size("ty")
    total_rows = lax.axis_size(("dx", "dc")) * lax.axis_size(("tx", "ty")) * rows
    scale = float(total_rows) ** (-0.5)

    boundary = shifted_by(block_input[rows - near :], ("tx", "ty"), 1)
    extended = jnp.concatenate([boundary, block_input], 0)
    near_input = extended[:rows]
    middle, first_tanh, first_gate, first_gated = causal_parts(
        block_input, near_input, first_conv_weight, first_residual_projection
    )
    far_input = shifted_by(middle, ("tx", "ty"), far_steps)
    other_one = from_pair(jnp.concatenate([extended, first_gated], 0))
    out_keep, out_send = halves_of(core, output_gradient[:, :half], output_gradient[:, half:])
    block_output, second_tanh, second_gate, second_gated = causal_parts(
        middle, far_input, second_conv_weight, second_residual_projection
    )
    other_two = from_pair(jnp.concatenate([far_input, middle, second_gated, out_send], 1))

    tanh_two, gate_two = grad_halves(
        second_tanh, second_gate, output_gradient, second_residual_projection
    )
    keep_two, send_two = halves_of(core, tanh_two, gate_two)
    other_pre_two = from_pair(send_two)
    pre_two = jnp.concatenate([tanh_two, gate_two], 1)
    tap_two = mult_trans(pre_two, second_conv_weight[:, : 2 * width]).astype(BF16)
    tap_two = shifted_by(tap_two, ("tx", "ty"), -far_steps)

    wide_pre = jnp.concatenate([keep_two, other_pre_two], 0)
    tap_sum = contract_rows(jnp.concatenate([far_input, other_two[:, :width]], 0), wide_pre).astype(BF16)
    now_sum = contract_rows(jnp.concatenate([middle, other_two[:, width : 2 * width]], 0), wide_pre).astype(BF16)
    proj_sum = contract_rows(
        jnp.concatenate([second_gated, other_two[:, 2 * width : 3 * width]], 0),
        jnp.concatenate([out_keep, other_two[:, 3 * width :]], 0),
    ).astype(BF16)
    tap_two, tap_sum, now_sum, proj_sum = lax.optimization_barrier(
        (tap_two, tap_sum, now_sum, proj_sum)
    )
    rest_total_two = sum_late(jnp.concatenate([now_sum, proj_sum], 1))
    tap_total_two = sum_early(tap_sum)

    middle_gradient = output_gradient.astype(F32) + mult_trans(pre_two, second_conv_weight[:, 2 * width :])
    middle_gradient = (middle_gradient + tap_two.astype(F32)).astype(BF16)

    tanh_one, gate_one = grad_halves(first_tanh, first_gate, middle_gradient, first_residual_projection)
    keep_one, send_one = halves_of(core, tanh_one, gate_one)
    mid_keep, mid_send = halves_of(core, middle_gradient[:, :half], middle_gradient[:, half:])
    came_one = from_pair(jnp.concatenate([send_one, mid_send], 1))
    wide_pre = jnp.concatenate([keep_one, came_one[:, :width]], 0)
    tap_sum = contract_rows(jnp.concatenate([near_input, other_one[:rows]], 0), wide_pre).astype(BF16)
    now_sum = contract_rows(
        jnp.concatenate([block_input, other_one[near : near + rows]], 0), wide_pre
    ).astype(BF16)
    proj_sum = contract_rows(
        jnp.concatenate([first_gated, other_one[near + rows :]], 0),
        jnp.concatenate([mid_keep, came_one[:, width:]], 0),
    ).astype(BF16)
    gathered_two = gather_rows(tap_total_two, rest_total_two)
    tap_sum, now_sum, proj_sum, rest_total_two = lax.optimization_barrier(
        (tap_sum, now_sum, proj_sum, rest_total_two)
    )
    rest_total_one = sum_late(jnp.concatenate([now_sum, proj_sum], 1))
    tap_total_one = sum_early(tap_sum)
    gathered_one = gather_rows(tap_total_one, rest_total_one)

    pre_one = jnp.concatenate([tanh_one, gate_one], 1)
    tap_one = mult_trans(pre_one, first_conv_weight[:, : 2 * width]).astype(BF16)
    tap_one = jnp.concatenate([tap_one[near:], shifted_by(tap_one[:near], ("tx", "ty"), -1)], 0)
    input_gradient = middle_gradient.astype(F32) + mult_trans(pre_one, first_conv_weight[:, 2 * width :])
    input_gradient = (input_gradient + tap_one.astype(F32)).astype(BF16)

    conv_two, proj_two = finish(core, scale, gathered_two, width)
    conv_one, proj_one = finish(core, scale, gathered_one, width)
    return (block_output[None], input_gradient[None], conv_one, proj_one, conv_two, proj_two)


def solution(mesh):
    streams, outer, inner = (mesh.shape[name] for name in ("dp", "tx", "ty"))
    fine = Mesh(
        mesh.devices.reshape(streams // 2, 2, outer, inner), ("dx", "dc", "tx", "ty")
    )
    data = P(("dx", "dc"), ("tx", "ty"), None)
    return jax.shard_map(
        shards,
        mesh=fine,
        in_specs=(data, P(), P(), P(), P(), data),
        out_specs=(data, data, P("ty", None), P("ty", None), P("ty", None), P("ty", None)),
        check_vma=False,
    )
```

```python
import jax
import jax.numpy as jnp
from jax import lax
from jax.sharding import Mesh
from jax.sharding import PartitionSpec as P

NEAR_DILATION = 64
BF16 = jnp.bfloat16
F32 = jnp.float32


def shifted_by(value, axis, steps):
    count = lax.axis_size(axis)
    leading, last = (max(0, -steps), min(count, count - steps))
    return lax.ppermute(value, axis, [(source, source + steps) for source in range(leading, last)])


def from_pair(value):
    return lax.ppermute(value, "dc", [(0, 1), (1, 0)])


def mult_trans(left, right):
    return lax.dot_general(left, right, (((1,), (1,)), ((), ())), preferred_element_type=F32)


def contract_rows(left, right):
    return lax.dot_general(left, right, (((0,), (0,)), ((), ())), preferred_element_type=F32)


def causal_parts(input_frames, shifted, conv_weight, proj_weight):
    width = input_frames.shape[1]
    pre = jnp.dot(shifted, conv_weight[:, : 2 * width], preferred_element_type=F32)
    pre = pre + jnp.dot(input_frames, conv_weight[:, 2 * width :], preferred_element_type=F32)
    tanh_part = jnp.tanh(pre[:, :width])
    gate_part = jax.nn.sigmoid(pre[:, width:])
    gated = (tanh_part * gate_part).astype(BF16)
    output = (
        input_frames.astype(F32) + jnp.dot(gated, proj_weight, preferred_element_type=F32)
    ).astype(BF16)
    return (output, tanh_part, gate_part, gated)


def grad_halves(tanh_part, gate_part, grad_out, proj_weight):
    grad_gated = mult_trans(grad_out, proj_weight)
    tanh_half = (grad_gated * gate_part * (1.0 - tanh_part * tanh_part)).astype(BF16)
    gate_half = (grad_gated * tanh_part * gate_part * (1.0 - gate_part)).astype(BF16)
    return tanh_half, gate_half


def halves_of(core, first, second):
    return jnp.where(core == 0, first, second), jnp.where(core == 0, second, first)


def exchange(pick, axis):
    count, place = lax.axis_size(axis), lax.axis_index(axis)
    total = None
    for step in range(1, count):
        sent = pick((place + step) % count).astype(BF16)
        came = lax.ppermute(sent, axis, [(i, (i + step) % count) for i in range(count)])
        total = came.astype(F32) if total is None else total + came.astype(F32)
    return pick(place).astype(F32) + total


def part_of(value, place, count):
    rows = value.shape[-2] // count
    return lax.dynamic_slice_in_dim(value, place * rows, rows, value.ndim - 2)


def share_rows(value, axis):
    count = lax.axis_size(axis)
    return exchange(lambda place: part_of(value, place, count), axis)


def share_groups(value, axis):
    return exchange(lambda place: lax.dynamic_index_in_dim(value, place, 0, keepdims=False), axis)


def sum_inner_first(term):
    return share_rows(share_rows(term, "ty"), "dx")


def sum_outer_first(term):
    shares = lax.axis_size("ty")
    groups = term.reshape(shares, term.shape[0] // shares, term.shape[1])
    return share_groups(share_rows(groups, "dx"), "ty")


def gather(value, axis):
    count = lax.axis_size(axis)
    parts = [value]
    for step in range(1, count):
        parts.append(lax.ppermute(value, axis, [(i, (i + step) % count) for i in range(count)]))
    return parts


def sum_gather(part):
    piece = share_rows(part, "tx").astype(BF16)
    return jnp.stack(gather(jnp.concatenate(gather(piece, "tx"), 0), "dx"), 0)


def in_order(value, count, axis):
    place = lax.axis_index(axis)
    return jnp.stack(
        [lax.dynamic_index_in_dim(value, (place - i) % count, 0, keepdims=False) for i in range(count)], 0
    )


def whole_rows(value):
    outer, rest = lax.axis_size("dx"), lax.axis_size("tx")
    columns = value.shape[-1]
    rows = value.shape[1] // rest
    value = value.reshape(outer, rest, rows, columns).swapaxes(0, 1)
    value = in_order(value, rest, "tx").swapaxes(0, 1)
    return in_order(value, outer, "dx").reshape(outer * rest * rows, columns)


def finish(core, scale, tap, now, proj):
    pairs = []
    for mine in (tap, now, proj):
        other = from_pair(mine)
        first, second = halves_of(core, mine, other)
        pairs.append(jnp.concatenate([whole_rows(first), whole_rows(second)], 1))
    conv = jnp.concatenate(pairs[:2], 1)
    return conv.astype(F32) * scale, pairs[2].astype(F32) * scale


def shards(
    frames,
    first_conv_weight,
    first_residual_projection,
    second_conv_weight,
    second_residual_projection,
    out_grad,
):
    near = NEAR_DILATION
    block_input = frames[0]
    output_gradient = out_grad[0]
    rows, width = block_input.shape
    half = width // 2
    core = lax.axis_index("dc")
    far_steps = lax.axis_size("ty")
    total_rows = lax.axis_size(("dx", "dc")) * lax.axis_size(("tx", "ty")) * rows
    scale = float(total_rows) ** (-0.5)

    boundary = shifted_by(block_input[rows - near :], ("tx", "ty"), 1)
    extended = jnp.concatenate([boundary, block_input], 0)
    near_input = extended[:rows]
    middle, first_tanh, first_gate, first_gated = causal_parts(
        block_input, near_input, first_conv_weight, first_residual_projection
    )
    far_input = shifted_by(middle, ("tx", "ty"), far_steps)
    other_one = from_pair(jnp.concatenate([extended, first_gated], 0))
    out_keep, out_send = halves_of(core, output_gradient[:, :half], output_gradient[:, half:])
    block_output, second_tanh, second_gate, second_gated = causal_parts(
        middle, far_input, second_conv_weight, second_residual_projection
    )
    other_two = from_pair(jnp.concatenate([far_input, middle, second_gated, out_send], 1))

    tanh_two, gate_two = grad_halves(
        second_tanh, second_gate, output_gradient, second_residual_projection
    )
    keep_two, send_two = halves_of(core, tanh_two, gate_two)
    other_pre_two = from_pair(send_two)
    pre_two = jnp.concatenate([tanh_two, gate_two], 1)
    tap_two = mult_trans(pre_two, second_conv_weight[:, : 2 * width]).astype(BF16)
    tap_two = shifted_by(tap_two, ("tx", "ty"), -far_steps)

    proj_sum = contract_rows(
        jnp.concatenate([second_gated, other_two[:, 2 * width : 3 * width]], 0),
        jnp.concatenate([out_keep, other_two[:, 3 * width :]], 0),
    ).astype(BF16)
    wide_pre = jnp.concatenate([keep_two, other_pre_two], 0)
    tap_sum = contract_rows(jnp.concatenate([far_input, other_two[:, :width]], 0), wide_pre).astype(BF16)
    now_sum = contract_rows(jnp.concatenate([middle, other_two[:, width : 2 * width]], 0), wide_pre).astype(BF16)
    tap_two, tap_sum, now_sum, proj_sum = lax.optimization_barrier(
        (tap_two, tap_sum, now_sum, proj_sum)
    )
    proj_part_two = sum_inner_first(proj_sum)
    tap_part_two = sum_inner_first(tap_sum)
    now_part_two = sum_outer_first(now_sum)

    middle_gradient = output_gradient.astype(F32) + mult_trans(pre_two, second_conv_weight[:, 2 * width :])
    middle_gradient = (middle_gradient + tap_two.astype(F32)).astype(BF16)

    tanh_one, gate_one = grad_halves(first_tanh, first_gate, middle_gradient, first_residual_projection)
    keep_one, send_one = halves_of(core, tanh_one, gate_one)
    mid_keep, mid_send = halves_of(core, middle_gradient[:, :half], middle_gradient[:, half:])
    came_one = from_pair(jnp.concatenate([send_one, mid_send], 1))
    wide_pre = jnp.concatenate([keep_one, came_one[:, :width]], 0)
    tap_sum = contract_rows(jnp.concatenate([near_input, other_one[:rows]], 0), wide_pre).astype(BF16)
    now_sum = contract_rows(
        jnp.concatenate([block_input, other_one[near : near + rows]], 0), wide_pre
    ).astype(BF16)
    proj_sum = contract_rows(
        jnp.concatenate([first_gated, other_one[near + rows :]], 0),
        jnp.concatenate([mid_keep, came_one[:, width:]], 0),
    ).astype(BF16)
    proj_total_two = sum_gather(proj_part_two)
    tap_total_two = sum_gather(tap_part_two)
    now_total_two = sum_gather(now_part_two)
    proj_total_one = sum_gather(sum_inner_first(proj_sum))
    tap_total_one = sum_gather(sum_inner_first(tap_sum))
    now_total_one = sum_gather(sum_outer_first(now_sum))

    pre_one = jnp.concatenate([tanh_one, gate_one], 1)
    tap_one = mult_trans(pre_one, first_conv_weight[:, : 2 * width]).astype(BF16)
    tap_one = jnp.concatenate([tap_one[near:], shifted_by(tap_one[:near], ("tx", "ty"), -1)], 0)
    input_gradient = middle_gradient.astype(F32) + mult_trans(pre_one, first_conv_weight[:, 2 * width :])
    input_gradient = (input_gradient + tap_one.astype(F32)).astype(BF16)

    conv_two, proj_two = finish(core, scale, tap_total_two, now_total_two, proj_total_two)
    conv_one, proj_one = finish(core, scale, tap_total_one, now_total_one, proj_total_one)
    return (block_output[None], input_gradient[None], conv_one, proj_one, conv_two, proj_two)


def solution(mesh):
    streams, outer, inner = (mesh.shape[name] for name in ("dp", "tx", "ty"))
    fine = Mesh(
        mesh.devices.reshape(streams // 2, 2, outer, inner), ("dx", "dc", "tx", "ty")
    )
    data = P(("dx", "dc"), ("tx", "ty"), None)
    return jax.shard_map(
        shards,
        mesh=fine,
        in_specs=(data, P(), P(), P(), P(), data),
        out_specs=(data, data, P("ty", None), P("ty", None), P("ty", None), P("ty", None)),
        check_vma=False,
    )
```

```python
import jax
import jax.numpy as jnp
from jax import lax
from jax.sharding import Mesh
from jax.sharding import PartitionSpec as P

NEAR_DILATION = 64
BF16 = jnp.bfloat16
F32 = jnp.float32


def shifted_by(value, axis, steps):
    count = lax.axis_size(axis)
    leading, last = (max(0, -steps), min(count, count - steps))
    return lax.ppermute(value, axis, [(source, source + steps) for source in range(leading, last)])


def from_pair(value):
    return lax.ppermute(value, "dc", [(0, 1), (1, 0)])


def mult_trans(left, right):
    return lax.dot_general(left, right, (((1,), (1,)), ((), ())), preferred_element_type=F32)


def contract_rows(left, right):
    return lax.dot_general(left, right, (((0,), (0,)), ((), ())), preferred_element_type=F32)


def causal_parts(input_frames, shifted, conv_weight, proj_weight):
    width = input_frames.shape[1]
    pre = jnp.dot(shifted, conv_weight[:, : 2 * width], preferred_element_type=F32)
    pre = pre + jnp.dot(input_frames, conv_weight[:, 2 * width :], preferred_element_type=F32)
    tanh_part = jnp.tanh(pre[:, :width])
    gate_part = jax.nn.sigmoid(pre[:, width:])
    gated = (tanh_part * gate_part).astype(BF16)
    output = (
        input_frames.astype(F32) + jnp.dot(gated, proj_weight, preferred_element_type=F32)
    ).astype(BF16)
    return (output, tanh_part, gate_part, gated)


def grad_halves(tanh_part, gate_part, grad_out, proj_weight):
    grad_gated = mult_trans(grad_out, proj_weight)
    tanh_half = (grad_gated * gate_part * (1.0 - tanh_part * tanh_part)).astype(BF16)
    gate_half = (grad_gated * tanh_part * gate_part * (1.0 - gate_part)).astype(BF16)
    return tanh_half, gate_half


def halves_of(core, first, second):
    return jnp.where(core == 0, first, second), jnp.where(core == 0, second, first)


def part_of(value, place, count):
    rows = value.shape[0] // count
    return lax.dynamic_slice_in_dim(value, place * rows, rows, 0)


def pick(value, place):
    return lax.dynamic_index_in_dim(value, place, 0, keepdims=False)


def plus(*terms):
    total = terms[0].astype(F32)
    for term in terms[1:]:
        total = total + term.astype(F32)
    return total.astype(BF16)


def swap(value, axis, apart=1):
    count = lax.axis_size(axis)
    return lax.ppermute(value, axis, [(i, i ^ apart) for i in range(count)])


class Order:
    def __init__(self):
        self.last = None

    def __call__(self, step, *inputs):
        if self.last is not None:
            inputs, unused = lax.optimization_barrier((inputs, self.last))
        outputs = step(*inputs)
        self.last = outputs[0] if isinstance(outputs, tuple) else outputs
        return outputs


class Stream:
    def __init__(self, order, inner_first):
        self.order, self.inner_first = order, inner_first
        self.x, self.y, self.z = (lax.axis_index(name) for name in ("dx", "ty", "tx"))
        self.low, self.high = self.z % 2, self.z // 2
        self.shares = lax.axis_size("ty")

    def begin(self, make, *inputs):
        shares = self.shares

        def step(*inputs):
            term = make(*inputs)
            if self.inner_first:
                return part_of(term, 1 - self.y, 2), term
            groups = term.reshape(shares, 2, term.shape[0] // (2 * shares), term.shape[1])
            return lax.dynamic_index_in_dim(groups, 1 - self.x, 1, keepdims=False), groups

        if self.inner_first and shares != 2:
            term = self.order(make, *inputs)
            self.kept = lax.psum_scatter(term, "ty", scatter_dimension=0, tiled=True)
            return
        sent, self.kept = self.order(step, *inputs)
        self.came = swap(sent, "ty" if self.inner_first else "dx")

    def second(self):
        if self.inner_first and self.shares != 2:
            sent, self.kept = self.order(
                lambda kept: (part_of(kept, 1 - self.x, 2), part_of(kept, self.x, 2)), self.kept
            )
            self.came = swap(sent, "dx")
            return
        if self.inner_first:

            def step(term, came):
                rows = plus(part_of(term, self.y, 2), came)
                return part_of(rows, 1 - self.x, 2), part_of(rows, self.x, 2)

            sent, self.kept = self.order(step, self.kept, self.came)
            self.came = swap(sent, "dx")
            return
        if self.shares != 2:
            rows = self.order(
                lambda groups, came: plus(
                    lax.dynamic_index_in_dim(groups, self.x, 1, keepdims=False), came
                ),
                self.kept,
                self.came,
            )
            self.kept = lax.psum_scatter(rows, "ty", scatter_dimension=0, tiled=False)
            self.came = jnp.zeros_like(self.kept)
            return

        def step(groups, came):
            rows = plus(lax.dynamic_index_in_dim(groups, self.x, 1, keepdims=False), came)
            return pick(rows, 1 - self.y), pick(rows, self.y)

        sent, self.kept = self.order(step, self.kept, self.came)
        self.came = swap(sent, "ty")

    def third(self):
        def step(kept, came):
            rows = plus(kept, came)
            fours = rows.reshape(2, 2, rows.shape[0] // 4, rows.shape[1])
            sent = lax.dynamic_index_in_dim(fours, 1 - self.low, 1, keepdims=False)
            return sent, lax.dynamic_index_in_dim(fours, self.low, 1, keepdims=False)

        sent, self.kept = self.order(step, self.kept, self.came)
        self.came = swap(sent, "tx")

    def fourth(self):
        def step(kept, came):
            rows = plus(kept, came)
            return pick(rows, 1 - self.high), pick(rows, self.high)

        sent, self.kept = self.order(step, self.kept, self.came)
        self.came = swap(sent, "tx", 2)

    def fifth(self):
        self.own = self.order(plus, self.kept, self.came)
        self.two = swap(self.own, "tx", 2)
        self.one = swap(self.own, "tx")
        self.three = swap(self.two, "tx")

    def sixth(self):
        def step(own, one, two, three):
            near, far = jnp.concatenate(halves_of(self.low, own, one), 0), jnp.concatenate(halves_of(self.low, two, three), 0)
            return jnp.concatenate(halves_of(self.high, near, far), 0)

        self.rows = self.order(step, self.own, self.one, self.two, self.three)
        self.rows_x = swap(self.rows, "dx")
        self.core_rows = from_pair(self.rows)
        self.core_rows_x = from_pair(self.rows_x)


def finish(order, core, scale, tap, now, proj):
    def whole(core, x, rows, rows_x, core_rows, core_rows_x):
        mine = jnp.concatenate(halves_of(x, rows, rows_x), 0)
        other = jnp.concatenate(halves_of(x, core_rows, core_rows_x), 0)
        return jnp.concatenate(halves_of(core, mine, other), 1)

    def step(*values):
        values = list(values)
        out = [whole(core, tap.x, *values[i : i + 4]) for i in range(0, len(values), 4)]
        return jnp.concatenate(out, 1).astype(F32) * scale

    def four(stream):
        return (stream.rows, stream.rows_x, stream.core_rows, stream.core_rows_x)

    proj_out = order(step, *four(proj))
    return order(step, *four(tap), *four(now)), proj_out


def shards(
    frames,
    first_conv_weight,
    first_residual_projection,
    second_conv_weight,
    second_residual_projection,
    out_grad,
):
    near = NEAR_DILATION
    block_input = frames[0]
    output_gradient = out_grad[0]
    rows, width = block_input.shape
    half = width // 2
    core = lax.axis_index("dc")
    far_steps = lax.axis_size("ty")
    total_rows = lax.axis_size(("dx", "dc")) * lax.axis_size(("tx", "ty")) * rows
    scale = float(total_rows) ** (-0.5)
    order = Order()

    last_rows = block_input[rows - near :]
    boundary = shifted_by(last_rows, ("tx", "ty"), 1)
    far_frames = shifted_by(block_input, ("tx", "ty"), far_steps)
    far_boundary = shifted_by(last_rows, ("tx", "ty"), far_steps + 1)
    extended = jnp.concatenate([boundary, block_input], 0)
    middle, first_tanh, first_gate, first_gated = causal_parts(
        block_input, extended[:rows], first_conv_weight, first_residual_projection
    )
    far_shifted = jnp.concatenate([far_boundary, far_frames[: rows - near]], 0)
    far_frames, far_shifted, middle = lax.optimization_barrier((far_frames, far_shifted, middle))
    far_input = causal_parts(far_frames, far_shifted, first_conv_weight, first_residual_projection)[0]
    block_output, second_tanh, second_gate, second_gated = causal_parts(
        middle, far_input, second_conv_weight, second_residual_projection
    )
    out_keep, out_send = halves_of(core, output_gradient[:, :half], output_gradient[:, half:])
    extended_other, first_gated_other = from_pair(extended), from_pair(first_gated)
    middle_other, far_other, second_gated_other, out_other = (
        from_pair(value) for value in (middle, far_input, second_gated, out_send)
    )

    def start_two(tanh, gate, grad_out):
        first, second = grad_halves(tanh, gate, grad_out, second_residual_projection)
        return (jnp.concatenate([first, second], 1),) + halves_of(core, first, second)

    pre_two, keep_two, send_two = order(start_two, second_tanh, second_gate, output_gradient)
    pre_two_other = from_pair(send_two)
    tap_two = order(
        lambda pre: mult_trans(pre, second_conv_weight[:, : 2 * width]).astype(BF16), pre_two
    )
    tap_two = shifted_by(tap_two, ("tx", "ty"), -far_steps)

    def product(left, left_other, right, right_other):
        left = jnp.concatenate([left, left_other], 0)
        right = jnp.concatenate([right, right_other], 0)
        return contract_rows(left, right).astype(BF16)

    streams = {
        name: Stream(order, inner_first)
        for name, inner_first in (
            ("p2", True), ("t2", True), ("n2", False), ("p1", True), ("t1", True), ("n1", False),
        )
    }
    streams["p2"].begin(product, second_gated, second_gated_other, out_keep, out_other)
    streams["t2"].begin(product, far_input, far_other, keep_two, pre_two_other)
    streams["n2"].begin(product, middle, middle_other, keep_two, pre_two_other)
    now_two = order(lambda pre: mult_trans(pre, second_conv_weight[:, 2 * width :]), pre_two)

    def start_one(tanh, gate, grad_out, now, tap):
        grad = (grad_out.astype(F32) + now + tap.astype(F32)).astype(BF16)
        first, second = grad_halves(tanh, gate, grad, first_residual_projection)
        keep, send = halves_of(core, first, second)
        grad_keep, grad_send = halves_of(core, grad[:, :half], grad[:, half:])
        return (jnp.concatenate([first, second], 1), keep, send, grad, grad_keep, grad_send)

    pre_one, keep_one, send_one, middle_gradient, mid_keep, mid_send = order(
        start_one, first_tanh, first_gate, output_gradient, now_two, tap_two
    )
    pre_one_other, mid_other = from_pair(send_one), from_pair(mid_send)

    def run(*names):
        for name in names:
            stream, stage = name.split(".")
            getattr(streams[stream], STAGES[int(stage)])()

    run("p2.2")
    streams["p1"].begin(product, first_gated, first_gated_other, mid_keep, mid_other)
    streams["t1"].begin(product, extended[:rows], extended_other[:rows], keep_one, pre_one_other)
    streams["n1"].begin(product, block_input, extended_other[near:], keep_one, pre_one_other)
    run("p2.3", "n2.2", "t2.2", "p2.4")
    tap_one = order(lambda pre: mult_trans(pre, first_conv_weight[:, : 2 * width]).astype(BF16), pre_one)
    tap_next = shifted_by(tap_one[:near], ("tx", "ty"), -1)
    run("p2.5", "t2.3", "n2.3", "p1.2")

    def last_grad(grad, pre, tap, tap_next):
        tap = jnp.concatenate([tap[near:], tap_next], 0)
        now = mult_trans(pre, first_conv_weight[:, 2 * width :])
        return (grad.astype(F32) + now + tap.astype(F32)).astype(BF16)

    input_gradient = order(last_grad, middle_gradient, pre_one, tap_one, tap_next)
    run("t2.4", "n2.4", "p1.3", "p2.6", "t2.5", "n2.5", "n1.2", "t1.2", "p1.4", "t2.6", "n2.6", "p1.5")
    run("t1.3", "n1.3", "t1.4", "n1.4", "p1.6", "t1.5", "n1.5")
    conv_two, proj_two = finish(order, core, scale, streams["t2"], streams["n2"], streams["p2"])
    run("t1.6", "n1.6")
    conv_one, proj_one = finish(order, core, scale, streams["t1"], streams["n1"], streams["p1"])
    return (block_output[None], input_gradient[None], conv_one, proj_one, conv_two, proj_two)


STAGES = (None, "begin", "second", "third", "fourth", "fifth", "sixth")


def solution(mesh):
    streams, outer, inner = (mesh.shape[name] for name in ("dp", "tx", "ty"))
    fine = Mesh(
        mesh.devices.reshape(streams // 2, 2, outer, inner), ("dx", "dc", "tx", "ty")
    )
    data = P(("dx", "dc"), ("tx", "ty"), None)
    return jax.shard_map(
        shards,
        mesh=fine,
        in_specs=(data, P(), P(), P(), P(), data),
        out_specs=(data, data, P("ty", None), P("ty", None), P("ty", None), P("ty", None)),
        check_vma=False,
    )
```
